512 devices in a mesh: replica: 32 (over y, x), shard: 16 (over z, core).
Axes of the slice: x: 4, y: 8, z: 8, core: 2. Of those that a mesh axis runs over, the one named last changes fastest.
Arguments:
- grads: bfloat16 [32, 256, 8192], P('replica', 'shard'), may hold values from -6 to 6
- error: float32 [32, 256, 8192], P('replica', 'shard'), may hold values from -4 to 4
- momentum: float32 [256, 8192], P('shard'), may hold values from -1 to 1
- weight: bfloat16 [256, 8192], P('shard'), may hold values from -6 to 6
- q_start: float32 [8192, 32], replicated, may hold values from -6 to 6
Outputs:
- new_error: float32 [32, 256, 8192], P('replica', 'shard')
- new_momentum: float32 [256, 8192], P('shard')
- new_weight: bfloat16 [256, 8192], P('shard')
- q_next: float32 [8192, 32], replicated
The draws below stay inside these ranges and needn't reach their ends.
All inputs are finite; a program needn't handle non-finite values.
Results may differ from the reference program's by a relative error of at most 0.001.
Values sent between devices are 32-bit elements; how exact they have to be, the bound alone decides.
A program may use at most 64 MiB of HBM per device.

```python
import jax
import jax.numpy as jnp
from jax import lax

D = 8192
RANK = 32
ROWS = 256
REPL = 32
N_REPLICA = 32


def levels(key, extent, cuts, smallest, largest):
    factor_of, own = 1.0, jax.random.fold_in(key, 6)
    for position, parts in cuts:
        draws = jnp.exp(jax.random.uniform(jax.random.fold_in(own, position), (parts,), jnp.float32, smallest / len(cuts), largest / len(cuts)))
        factor_of = factor_of * jnp.repeat(draws, extent[position] // parts).reshape([-1 if axis == position else 1 for axis in range(len(extent))])
    return factor_of


def bell_draw(own_key, extent, deviation, limit, split=(), dtype=jnp.bfloat16):
    drawn = jax.random.normal(own_key, extent, jnp.float32) * deviation
    if len(split) > 0:
        drawn = levels(own_key, extent, split, -0.22, 0.18) * drawn
    return jnp.clip(drawn, min=-limit, max=limit).astype(dtype)


def setup_inputs(seed: int = 0) -> dict:
    key_list = jax.random.split(jax.random.key(seed), 6)
    grads = bell_draw(key_list[0], (REPL, ROWS, D), 1.0, 6.0, ((0, 32), (1, 16)))
    error = bell_draw(key_list[1], (REPL, ROWS, D), 0.5, 4.0, ((0, 32), (1, 16)), jnp.float32)
    momentum = bell_draw(key_list[2], (ROWS, D), 0.1, 1.0, ((0, 16),), jnp.float32)
    weight = bell_draw(key_list[3], (ROWS, D), 1.0, 6.0, ((0, 16),))
    q_start = bell_draw(key_list[4], (D, RANK), 1.0, 6.0, (), jnp.float32)
    return dict(grads=grads, error=error, momentum=momentum, weight=weight, q_start=q_start)


def reference(grads, error, momentum, weight, q_start):
    highest = lax.Precision.HIGHEST
    merged = grads.astype(jnp.float32) + error
    p_sum = jnp.einsum('rmd,dk->mk', merged, q_start, precision=highest)
    gram = jnp.dot(p_sum.T, p_sum, precision=highest)
    factor = jnp.linalg.cholesky(gram)
    p_ortho = jax.scipy.linalg.solve_triangular(factor, p_sum.T, lower=True).T
    q_total = jnp.einsum('rmd,mk->dk', merged, p_ortho, precision=highest)
    q_next = q_total / N_REPLICA
    approx = jnp.dot(p_ortho, q_next.T, precision=highest)
    new_error = merged - approx[None]
    new_momentum = 0.9 * momentum + approx
    new_weight = (weight.astype(jnp.float32) - 0.5 * new_momentum).astype(jnp.bfloat16)
    return (new_error, new_momentum, new_weight, q_next)
```

```python
import jax
import jax.numpy as jnp
from jax import lax
from jax.experimental import pallas as pl
from jax.experimental.pallas import tpu as pltpu
from jax.sharding import PartitionSpec as P

MESH = pl.DeviceIdType.MESH
HIGHEST = lax.Precision.HIGHEST
NX, NY, NZ, NC = 4, 8, 8, 2
RANK = 32
D = 8192
NT = (((1,), (1,)), ((), ()))


def send(src, dst, send_sem, recv_sem, device):
    copy = pltpu.make_async_remote_copy(
        src_ref=src, dst_ref=dst, send_sem=send_sem, recv_sem=recv_sem,
        device_id=device, device_id_type=MESH,
    )
    copy.start()
    return copy


def factor_rows(gram, pt, steps):
    sub = lax.broadcasted_iota(jnp.int32, (RANK, 1), 0)
    for j in steps:
        col = gram[:, j:j + 1]
        r = lax.rsqrt(gram[j:j + 1, j:j + 1])
        f = jnp.where(sub > j, col * r, 0.0)
        grow = gram[j:j + 1, :] * r
        prow = pt[j:j + 1, :] * r
        gram = gram - f * grow
        pt = jnp.where(sub == j, prow, pt - f * prow)
    return gram, pt


def kernel(grads, error, qs, qt, po, gbuf, ebuf, qsv, mbuf, s1buf, s1sum, s2buf, msum, mpair, mall,
           ploc, pxbuf, pxsum, pybuf, pall, oscr, load_sem, ssem, rsem):
    rep, shard = lax.axis_index("replica"), lax.axis_index("shard")
    x, y = lax.rem(rep, NX), lax.div(rep, NX)
    c, z = lax.rem(shard, NC), lax.div(shard, NC)

    def at_x(d):
        return (y * NX + lax.rem(x + d, NX), shard)

    def at_y(d):
        return (lax.rem(y + d, NY) * NX + x, shard)

    def at_z(d):
        return (rep, lax.rem(z + d, NZ) * NC + c)

    other = (rep, z * NC + (1 - c))

    slots = iter(range(64))

    def go(src, dst, device):
        k = next(slots)
        return send(src, dst, ssem.at[k], rsem.at[k], device)

    loads = []
    for g in range(NX):
        group = []
        for h in range(2):
            cols = pl.ds(h * 4096 + g * 1024, 1024)
            to = pl.ds(h * 1024, 1024)
            for i, (src, dst) in enumerate(((grads, gbuf), (error, ebuf), (qs, qsv))):
                cp = pltpu.make_async_copy(src.at[:, cols], dst.at[g, :, to], load_sem.at[g, h, i])
                cp.start()
                group.append(cp)
        loads.append(group)

    barrier = pltpu.get_barrier_semaphore()
    partners = [at_x(d) for d in range(1, NX)] + [at_y(d) for d in range(1, NY)] + [at_z(d) for d in range(1, NZ)] + [other]
    for device in partners:
        pl.semaphore_signal(barrier, inc=1, device_id=device, device_id_type=MESH)

    p = None
    for g in range(NX):
        for cp in loads[g]:
            cp.wait()
        m = gbuf[g].astype(jnp.float32) + ebuf[g]
        mbuf[g] = m
        t = lax.dot_general(m, qsv[g], NT, precision=HIGHEST, preferred_element_type=jnp.float32)
        p = t if p is None else p + t
    zero = jnp.zeros((8, 64), jnp.float32)
    packed = jnp.concatenate([p[0:8], p[8:16], zero], axis=1)
    ploc[...] = packed

    pl.semaphore_wait(barrier, len(partners))
    px = [go(ploc, pxbuf.at[x], at_x(d)) for d in range(1, NX)]
    s1 = [go(mbuf.at[lax.rem(x + d, NX)], s1buf.at[d - 1], at_x(d)) for d in range(1, NX)]

    pxbuf[x] = packed
    for cp in px:
        cp.wait_recv()
    packed = (pxbuf[0] + pxbuf[1]) + (pxbuf[2] + pxbuf[3])
    pxsum[...] = packed
    py = [go(pxsum, pybuf.at[y], at_y(d)) for d in range(1, NY)]
    pybuf[y] = packed
    for cp in py:
        cp.wait_recv()
    packed = ((pybuf[0] + pybuf[1]) + (pybuf[2] + pybuf[3])) + ((pybuf[4] + pybuf[5]) + (pybuf[6] + pybuf[7]))
    pall[z, c] = packed
    pc = go(pall.at[z, c], pall.at[z, c], other)

    for cp in s1:
        cp.wait_recv()
    for k in range(NY):
        for h in range(2):
            cols = pl.ds(h * 1024 + k * 128, 128)
            s1sum[k, h] = (mbuf[x, :, cols] + s1buf[0, :, cols]) + (s1buf[1, :, cols] + s1buf[2, :, cols])
    s2 = [go(s1sum.at[lax.rem(y + d, NY)], s2buf.at[d - 1], at_y(d)) for d in range(1, NY)]

    pc.wait_recv()
    pz = [go(pall.at[z], pall.at[z], at_z(d)) for d in range(1, NZ)]

    for cp in s2:
        cp.wait_recv()
    total = s1sum[y]
    for k in range(NY - 1):
        total = total + s2buf[k]
    msum[...] = total
    mpair[c] = msum[c]
    s3c = go(msum.at[1 - c], mpair.at[c], other)

    for cp in pz:
        cp.wait_recv()
    pt = pall[...].reshape(128, 128).T
    p0, p1 = pt[0:RANK], pt[RANK:2 * RANK]
    gram = (lax.dot_general(p0, p0, NT, precision=HIGHEST, preferred_element_type=jnp.float32)
            + lax.dot_general(p1, p1, NT, precision=HIGHEST, preferred_element_type=jnp.float32))
    pt = jnp.concatenate([p0, p1], axis=1)

    s3c.wait_recv()
    mall[z] = mpair[...]
    s3z = [go(mpair, mall.at[z], at_z(d)) for d in range(1, NZ)]
    gram, pt = factor_rows(gram, pt, range(RANK))

    for cp in s3z:
        cp.wait_recv()
    m0 = mall[:, :, 0:8, :].reshape(128, 128)
    m1 = mall[:, :, 8:16, :].reshape(128, 128)
    q = (jnp.dot(pt[:, 0:128], m0, precision=HIGHEST, preferred_element_type=jnp.float32)
         + jnp.dot(pt[:, 128:256], m1, precision=HIGHEST, preferred_element_type=jnp.float32)) * (1.0 / 32.0)

    half = c * 4096
    mine = pl.ds(pl.multiple_of(half + x * 1024 + y * 128, 128), 128)
    qt[:, mine] = q
    qy = [go(qt.at[:, mine], qt.at[:, mine], at_y(d)) for d in range(1, NY)]
    ot = jnp.concatenate([pt[:, 0:128], pt[:, 128:256]], axis=0)
    oscr[...] = jnp.concatenate([ot, jnp.zeros((64, 128), jnp.float32)], axis=0).T
    own = oscr[pl.ds(pl.multiple_of(shard * 8, 8), 8), :]
    po[0:8, :] = own[:, 0:RANK]
    po[8:16, :] = own[:, RANK:2 * RANK]
    for cp in qy:
        cp.wait_recv()
    mine = pl.ds(pl.multiple_of(half + x * 1024, 128), 1024)
    qx = [go(qt.at[:, mine], qt.at[:, mine], at_x(d)) for d in range(1, NX)]
    qc = [go(qt.at[:, mine], qt.at[:, mine], other)]
    for d in range(1, NX):
        qx[d - 1].wait_recv()
        theirs = pl.ds(pl.multiple_of(half + lax.rem(x + NX - d, NX) * 1024, 128), 1024)
        qc.append(go(qt.at[:, theirs], qt.at[:, theirs], other))
    for cp in qc:
        cp.wait_recv()
    for cp in px + s1 + py + [pc] + s2 + pz + [s3c] + s3z + qy + qx + qc:
        cp.wait_send()


def on_device(grads, error, momentum, weight, q_start):
    f32 = jnp.float32
    rows = grads.shape[1]
    vmem = pltpu.VMEM
    qt, p_ortho = pl.pallas_call(
        kernel,
        out_shape=(jax.ShapeDtypeStruct((RANK, D), f32), jax.ShapeDtypeStruct((rows, RANK), f32)),
        in_specs=[pl.BlockSpec(memory_space=pl.ANY)] * 3,
        out_specs=[pl.BlockSpec(memory_space=pltpu.VMEM)] * 2,
        scratch_shapes=[
            vmem((NX, rows, 2048), jnp.bfloat16),
            vmem((NX, rows, 2048), f32),
            vmem((NX, RANK, 2048), f32),
            vmem((NX, rows, 2048), f32),
            vmem((NX - 1, rows, 2048), f32),
            vmem((NY, NC, rows, 128), f32),
            vmem((NY - 1, NC, rows, 128), f32),
            vmem((NC, rows, 128), f32),
            vmem((NC, rows, 128), f32),
            vmem((NZ, NC, rows, 128), f32),
            vmem((8, 128), f32),
            vmem((NX, 8, 128), f32),
            vmem((8, 128), f32),
            vmem((NY, 8, 128), f32),
            vmem((NZ, NC, 8, 128), f32),
            vmem((128, 128), f32),
            pltpu.SemaphoreType.DMA((NX, 2, 3)),
            pltpu.SemaphoreType.DMA((64,)),
            pltpu.SemaphoreType.DMA((64,)),
        ],
        compiler_params=pltpu.CompilerParams(collective_id=0, has_side_effects=True, vmem_limit_bytes=24 * 2**20),
        name="reduce_factor_gather",
    )(grads[0], error[0], q_start.T)
    approx = jnp.dot(p_ortho, qt, precision=HIGHEST)
    merged = grads[0].astype(f32) + error[0]
    new_error = (merged - approx)[None]
    new_momentum = 0.9 * momentum + approx
    new_weight = (weight.astype(f32) - 0.5 * new_momentum).astype(jnp.bfloat16)
    return (new_error, new_momentum, new_weight, qt.T)


def solution(mesh):
    placed = (
        P("replica", "shard", None),
        P("replica", "shard", None),
        P("shard", None),
        P("shard", None),
        P(),
    )
    return jax.shard_map(
        on_device,
        mesh=mesh,
        in_specs=placed,
        out_specs=(P("replica", "shard", None), P("shard", None), P("shard", None), P()),
        check_vma=False,
    )
```

```python
import jax
import jax.numpy as jnp
from jax import lax
from jax.experimental import pallas as pl
from jax.experimental.pallas import tpu as pltpu
from jax.sharding import PartitionSpec as P

MESH = pl.DeviceIdType.MESH
HIGHEST = lax.Precision.HIGHEST
NX, NY, NZ, NC = 4, 8, 8, 2
RANK = 32
D = 8192
NT = (((1,), (1,)), ((), ()))


def send(src, dst, send_sem, recv_sem, device):
    copy = pltpu.make_async_remote_copy(
        src_ref=src, dst_ref=dst, send_sem=send_sem, recv_sem=recv_sem,
        device_id=device, device_id_type=MESH,
    )
    copy.start()
    return copy


def factor_rows(gram, pt, steps):
    sub = lax.broadcasted_iota(jnp.int32, (RANK, 1), 0)
    for j in steps:
        col = gram[:, j:j + 1]
        r = lax.rsqrt(gram[j:j + 1, j:j + 1])
        f = jnp.where(sub > j, col * r, 0.0)
        grow = gram[j:j + 1, :] * r
        prow = pt[j:j + 1, :] * r
        gram = gram - f * grow
        pt = jnp.where(sub == j, prow, pt - f * prow)
    return gram, pt


def kernel(grads, error, qs, qt, po, gbuf, ebuf, qsv, mbuf, s1buf, relay, passed, s1sum, s2buf, msum, mpair, mall,
           ploc, pysum, pxbuf, pybuf, pall, oscr, load_sem, ssem, rsem):
    rep, shard = lax.axis_index("replica"), lax.axis_index("shard")
    x, y = lax.rem(rep, NX), lax.div(rep, NX)
    c, z = lax.rem(shard, NC), lax.div(shard, NC)

    def at_x(d):
        return (y * NX + lax.rem(x + d, NX), shard)

    def at_y(d):
        return (lax.rem(y + d, NY) * NX + x, shard)

    def at_z(d):
        return (rep, lax.rem(z + d, NZ) * NC + c)

    other = (rep, z * NC + (1 - c))

    barrier = pltpu.get_barrier_semaphore()
    partners = [at_x(d) for d in range(1, NX)] + [at_y(d) for d in range(1, NY)] + [at_z(d) for d in range(1, NZ)] + [other]
    for device in partners:
        pl.semaphore_signal(barrier, inc=1, device_id=device, device_id_type=MESH)

    slots = iter(range(128))
    started = []

    def go(src, dst, device):
        k = next(slots)
        copy = send(src, dst, ssem.at[k], rsem.at[k], device)
        started.append(copy)
        return copy

    ahead = [lax.rem(x + d, NX) for d in range(NX)]
    order = (2, 1, 3, 0)

    def load(src, dst, k, g):
        group = []
        for h in range(2):
            cols = pl.ds(pl.multiple_of(h * 4096 + g * 1024, 1024), 1024)
            cp = pltpu.make_async_copy(src.at[:, cols], dst.at[g, :, pl.ds(h * 1024, 1024)], load_sem.at[k, h])
            cp.start()
            group.append(cp)
        return group

    mloads = [load(grads, gbuf, i, ahead[d]) + load(error, ebuf, 4 + i, ahead[d]) for i, d in enumerate(order)]
    qloads = [load(qs, qsv, 8 + i, ahead[d]) for i, d in enumerate(order)]
    for i, d in enumerate(order):
        for cp in mloads[i]:
            cp.wait()
        mbuf[ahead[d]] = gbuf[ahead[d]].astype(jnp.float32) + ebuf[ahead[d]]

    lo, hi = pl.ds(0, 8), pl.ds(8, 8)
    pl.semaphore_wait(barrier, len(partners))
    right_relay = go(mbuf.at[ahead[2], lo], relay.at[0], at_x(1))
    left_relay = go(mbuf.at[ahead[2], hi], relay.at[1], at_x(3))
    right_own = go(mbuf.at[ahead[1], hi], s1buf.at[0, hi], at_x(1))
    left_own = go(mbuf.at[ahead[3], lo], s1buf.at[1, lo], at_x(3))

    p = None
    for i, d in enumerate(order):
        for cp in qloads[i]:
            cp.wait()
        t = lax.dot_general(mbuf[ahead[d]], qsv[ahead[d]], NT, precision=HIGHEST, preferred_element_type=jnp.float32)
        p = t if p is None else p + t
    packed = jnp.concatenate([p[0:8], p[8:16], jnp.zeros((8, 64), jnp.float32)], axis=1)
    ploc[...] = packed
    py = [go(ploc, pybuf.at[y], at_y(d)) for d in range(1, NY)]
    pybuf[y] = packed

    right_relay.wait_recv()
    passed[0] = mbuf[ahead[1], lo] + relay[0]
    right_sum = go(passed.at[0], s1buf.at[0, lo], at_x(1))
    left_relay.wait_recv()
    passed[1] = mbuf[ahead[3], hi] + relay[1]
    left_sum = go(passed.at[1], s1buf.at[1, hi], at_x(3))

    for cp in py:
        cp.wait_recv()
    packed = ((pybuf[0] + pybuf[1]) + (pybuf[2] + pybuf[3])) + ((pybuf[4] + pybuf[5]) + (pybuf[6] + pybuf[7]))
    pysum[...] = packed
    px = [go(pysum, pxbuf.at[x], at_x(d)) for d in range(1, NX)]
    pxbuf[x] = packed

    for cp in (right_own, left_own, right_sum, left_sum):
        cp.wait_recv()
    for k in range(NY):
        for h in range(2):
            cols = pl.ds(h * 1024 + k * 128, 128)
            s1sum[k, h] = mbuf[x, :, cols] + (s1buf[0, :, cols] + s1buf[1, :, cols])
    s2 = [go(s1sum.at[lax.rem(y + d, NY)], s2buf.at[d - 1], at_y(d)) for d in range(1, NY)]

    for cp in px:
        cp.wait_recv()
    pall[z, c] = (pxbuf[0] + pxbuf[1]) + (pxbuf[2] + pxbuf[3])
    pc = go(pall.at[z, c], pall.at[z, c], other)
    pc.wait_recv()
    pz = [go(pall.at[z], pall.at[z], at_z(d)) for d in range(1, NZ)]

    for cp in s2:
        cp.wait_recv()
    total = s1sum[y]
    for k in range(NY - 1):
        total = total + s2buf[k]
    msum[...] = total
    mpair[c] = msum[c]
    s3c = go(msum.at[1 - c], mpair.at[c], other)
    s3c.wait_recv()
    mall[z] = mpair[...]
    s3z = [go(mpair, mall.at[z], at_z(d)) for d in range(1, NZ)]

    for cp in pz:
        cp.wait_recv()
    pt = pall[...].reshape(128, 128).T
    p0, p1 = pt[0:RANK], pt[RANK:2 * RANK]
    gram = (lax.dot_general(p0, p0, NT, precision=HIGHEST, preferred_element_type=jnp.float32)
            + lax.dot_general(p1, p1, NT, precision=HIGHEST, preferred_element_type=jnp.float32))
    pt = jnp.concatenate([p0, p1], axis=1)
    gram, pt = factor_rows(gram, pt, range(RANK))
    ot = jnp.concatenate([pt[:, 0:128], pt[:, 128:256], jnp.zeros((64, 128), jnp.float32)], axis=0)
    oscr[...] = ot.T
    own = oscr[pl.ds(pl.multiple_of(shard * 8, 8), 8), :]
    po[0:8, :] = own[:, 0:RANK]
    po[8:16, :] = own[:, RANK:2 * RANK]

    for cp in s3z:
        cp.wait_recv()
    m0 = mall[:, :, 0:8, :].reshape(128, 128)
    m1 = mall[:, :, 8:16, :].reshape(128, 128)
    q = (jnp.dot(pt[:, 0:128], m0, precision=HIGHEST, preferred_element_type=jnp.float32)
         + jnp.dot(pt[:, 128:256], m1, precision=HIGHEST, preferred_element_type=jnp.float32)) * (1.0 / 32.0)

    def block(dx, dy):
        col = c * 4096 + lax.rem(x + dx, NX) * 1024 + lax.rem(y + dy, NY) * 128
        return pl.ds(pl.multiple_of(col, 128), 128)

    qt[:, block(0, 0)] = q

    def same(rows, cols, device):
        return go(qt.at[rows, cols], qt.at[rows, cols], device)

    every, top, low = pl.ds(0, RANK), pl.ds(0, RANK // 2), pl.ds(RANK // 2, RANK // 2)
    qy = {d: same(every, block(0, 0), at_y(d)) for d in (1, 7, 2, 6, 3, 5, 4)}
    arrivals = (0, 1, 7, 2, 6, 3, 5, 4)
    right, left, right_half, left_half = {}, {}, {}, {}
    for d in arrivals:
        if d:
            qy[d].wait_recv()
        right[d] = same(every, block(0, NY - d), at_x(1))
        left[d] = same(every, block(0, NY - d), at_x(3))
    group = pl.ds(pl.multiple_of(c * 4096 + x * 1024, 1024), 1024)
    qc = [same(every, group, other)]
    for d in arrivals:
        right[d].wait_recv()
        right_half[d] = same(top, block(3, NY - d), at_x(1))
        left[d].wait_recv()
        left_half[d] = same(low, block(1, NY - d), at_x(3))
    for dx in (1, 3, 2):
        if dx == 2:
            for d in arrivals:
                right_half[d].wait_recv()
                left_half[d].wait_recv()
        group = pl.ds(pl.multiple_of(c * 4096 + lax.rem(x + dx, NX) * 1024, 1024), 1024)
        qc.append(same(every, group, other))
    for cp in qc:
        cp.wait_recv()
    for cp in started:
        cp.wait_send()


def on_device(grads, error, momentum, weight, q_start):
    f32 = jnp.float32
    rows = grads.shape[1]
    vmem = pltpu.VMEM
    qt, p_ortho = pl.pallas_call(
        kernel,
        out_shape=(jax.ShapeDtypeStruct((RANK, D), f32), jax.ShapeDtypeStruct((rows, RANK), f32)),
        in_specs=[pl.BlockSpec(memory_space=pltpu.HBM)] * 3,
        out_specs=[pl.BlockSpec(memory_space=pltpu.VMEM)] * 2,
        scratch_shapes=[
            vmem((NX, rows, 2048), jnp.bfloat16),
            vmem((NX, rows, 2048), f32),
            vmem((NX, RANK, 2048), f32),
            vmem((NX, rows, 2048), f32),
            vmem((2, rows, 2048), f32),
            vmem((2, 8, 2048), f32),
            vmem((2, 8, 2048), f32),
            vmem((NY, NC, rows, 128), f32),
            vmem((NY - 1, NC, rows, 128), f32),
            vmem((NC, rows, 128), f32),
            vmem((NC, rows, 128), f32),
            vmem((NZ, NC, rows, 128), f32),
            vmem((8, 128), f32),
            vmem((8, 128), f32),
            vmem((NX, 8, 128), f32),
            vmem((NY, 8, 128), f32),
            vmem((NZ, NC, 8, 128), f32),
            vmem((128, 128), f32),
            pltpu.SemaphoreType.DMA((12, 2)),
            pltpu.SemaphoreType.DMA((96,)),
            pltpu.SemaphoreType.DMA((96,)),
        ],
        compiler_params=pltpu.CompilerParams(collective_id=0, has_side_effects=True, vmem_limit_bytes=24 * 2**20),
        name="reduce_factor_gather",
    )(*[pltpu.with_memory_space_constraint(a, pltpu.HBM) for a in (grads[0], error[0], q_start.T)])
    approx = jnp.dot(p_ortho, qt, precision=HIGHEST)
    merged = grads[0].astype(f32) + error[0]
    new_error = (merged - approx)[None]
    new_momentum = 0.9 * momentum + approx
    new_weight = (weight.astype(f32) - 0.5 * new_momentum).astype(jnp.bfloat16)
    return (new_error, new_momentum, new_weight, qt.T)


def solution(mesh):
    placed = (
        P("replica", "shard", None),
        P("replica", "shard", None),
        P("shard", None),
        P("shard", None),
        P(),
    )
    return jax.shard_map(
        on_device,
        mesh=mesh,
        in_specs=placed,
        out_specs=(P("replica", "shard", None), P("shard", None), P("shard", None), P()),
        check_vma=False,
    )
```

```python
import jax
import jax.numpy as jnp
from jax import lax
from jax.experimental import pallas as pl
from jax.experimental.pallas import tpu as pltpu
from jax.sharding import PartitionSpec as P

MESH = pl.DeviceIdType.MESH
HIGHEST = lax.Precision.HIGHEST
NX, NY, NZ, NC = 4, 8, 8, 2
RANK = 32
D = 8192
NT = (((1,), (1,)), ((), ()))
FAR8, FAR4 = (4, 3, 5, 2, 6, 1, 7), (2, 1, 3)
ORDER = (0, 1, 7, 2, 6, 3, 4, 5)


def send(src, dst, send_sem, recv_sem, device):
    copy = pltpu.make_async_remote_copy(
        src_ref=src, dst_ref=dst, send_sem=send_sem, recv_sem=recv_sem,
        device_id=device, device_id_type=MESH,
    )
    copy.start()
    return copy


def factor_rows(gram, pt, steps):
    sub = lax.broadcasted_iota(jnp.int32, (RANK, 1), 0)
    for j in steps:
        col = gram[:, j:j + 1]
        r = lax.rsqrt(gram[j:j + 1, j:j + 1])
        f = jnp.where(sub > j, col * r, 0.0)
        grow = gram[j:j + 1, :] * r
        prow = pt[j:j + 1, :] * r
        gram = gram - f * grow
        pt = jnp.where(sub == j, prow, pt - f * prow)
    return gram, pt


def kernel(grads, error, qs, qb, po, gbuf, ebuf, qsv, mbuf, s1buf, relay, passed, s1sum, s2buf, msum, mall,
           ploc, pysum, pxbuf, pybuf, pall, oscr, load_sem, ssem, rsem):
    rep, shard = lax.axis_index("replica"), lax.axis_index("shard")
    x, y = lax.rem(rep, NX), lax.div(rep, NX)
    c, z = lax.rem(shard, NC), lax.div(shard, NC)

    def at_x(d):
        return (y * NX + lax.rem(x + d, NX), shard)

    def at_y(d):
        return (lax.rem(y + d, NY) * NX + x, shard)

    def at_z(d):
        return (rep, lax.rem(z + d, NZ) * NC + c)

    def at_zc(d):
        return (rep, lax.rem(z + d, NZ) * NC + (1 - c))

    other = at_zc(0)

    slots = iter(range(128))
    started = []

    def go(src, dst, device):
        k = next(slots)
        copy = send(src, dst, ssem.at[k], rsem.at[k], device)
        started.append(copy)
        return copy

    ahead = [lax.rem(x + d, NX) for d in range(NX)]
    order = (2, 1, 3, 0)

    def load(src, dst, k, g):
        cp = pltpu.make_async_copy(src.at[:, pl.ds(pl.multiple_of(g * 2048, 2048), 2048)], dst.at[g], load_sem.at[k])
        cp.start()
        return cp

    mloads = [(load(grads, gbuf, i, ahead[d]), load(error, ebuf, 4 + i, ahead[d])) for i, d in enumerate(order)]
    qloads = [load(qs, qsv, 8 + i, ahead[d]) for i, d in enumerate(order)]

    barrier = pltpu.get_barrier_semaphore()
    partners = [at(d) for d in FAR8 for at in (at_y, at_z, at_zc)] + [at_x(d) for d in FAR4] + [other]
    for device in partners:
        pl.semaphore_signal(barrier, inc=1, device_id=device, device_id_type=MESH)

    p = None
    for i, d in enumerate(order):
        for cp in mloads[i]:
            cp.wait()
        m = gbuf[ahead[d]].astype(jnp.float32) + ebuf[ahead[d]]
        mbuf[ahead[d]] = m
        qloads[i].wait()
        t = lax.dot_general(m, qsv[ahead[d]], NT, precision=HIGHEST, preferred_element_type=jnp.float32)
        p = t if p is None else p + t
    packed = jnp.concatenate([p[0:8], p[8:16], jnp.zeros((8, 64), jnp.float32)], axis=1)
    ploc[...] = packed

    lo, hi = pl.ds(0, 8), pl.ds(8, 8)
    pl.semaphore_wait(barrier, len(partners))
    right_relay = go(mbuf.at[ahead[2], lo], relay.at[0], at_x(1))
    left_relay = go(mbuf.at[ahead[2], hi], relay.at[1], at_x(3))
    right_own = go(mbuf.at[ahead[1], hi], s1buf.at[0, hi], at_x(1))
    left_own = go(mbuf.at[ahead[3], lo], s1buf.at[1, lo], at_x(3))

    py = [go(ploc, pybuf.at[y], at_y(d)) for d in FAR8]
    pybuf[y] = packed

    right_relay.wait_recv()
    passed[0] = mbuf[ahead[1], lo] + relay[0]
    right_sum = go(passed.at[0], s1buf.at[0, lo], at_x(1))
    left_relay.wait_recv()
    passed[1] = mbuf[ahead[3], hi] + relay[1]
    left_sum = go(passed.at[1], s1buf.at[1, hi], at_x(3))

    for cp in py:
        cp.wait_recv()
    packed = ((pybuf[0] + pybuf[1]) + (pybuf[2] + pybuf[3])) + ((pybuf[4] + pybuf[5]) + (pybuf[6] + pybuf[7]))
    pysum[...] = packed
    px = [go(pysum, pxbuf.at[x], at_x(d)) for d in FAR4]
    pxbuf[x] = packed

    for cp in (right_own, left_own, right_sum, left_sum):
        cp.wait_recv()
    for k in range(NY):
        for h in range(2):
            cols = pl.ds(h * 1024 + k * 128, 128)
            s1sum[k, h] = mbuf[x, :, cols] + (s1buf[0, :, cols] + s1buf[1, :, cols])
    s2 = [go(s1sum.at[lax.rem(y + d, NY)], s2buf.at[d - 1], at_y(d)) for d in FAR8]

    for cp in px:
        cp.wait_recv()
    pall[z, c] = (pxbuf[0] + pxbuf[1]) + (pxbuf[2] + pxbuf[3])
    pz = [go(pall.at[z, c], pall.at[z, c], at(d)) for d in FAR8 for at in (at_zc, at_z)] + [go(pall.at[z, c], pall.at[z, c], other)]

    for cp in s2:
        cp.wait_recv()
    total = s1sum[y]
    for k in range(NY - 1):
        total = total + s2buf[k]
    msum[...] = total
    mall[z, c] = msum[c]
    s3 = [go(msum.at[h], mall.at[z, c], at(d)) for d in FAR8 for h, at in ((1 - c, at_zc), (c, at_z))]
    s3.append(go(msum.at[1 - c], mall.at[z, c], other))

    for cp in pz:
        cp.wait_recv()
    pt = pall[...].reshape(128, 128).T
    p0, p1 = pt[0:RANK], pt[RANK:2 * RANK]
    gram = (lax.dot_general(p0, p0, NT, precision=HIGHEST, preferred_element_type=jnp.float32)
            + lax.dot_general(p1, p1, NT, precision=HIGHEST, preferred_element_type=jnp.float32))
    pt = jnp.concatenate([p0, p1], axis=1)
    gram, pt = factor_rows(gram, pt, range(RANK))
    ot = jnp.concatenate([pt[:, 0:128], pt[:, 128:256], jnp.zeros((64, 128), jnp.float32)], axis=0)
    oscr[...] = ot.T
    own = oscr[pl.ds(pl.multiple_of(shard * 8, 8), 8), :]
    po[0:8, :] = own[:, 0:RANK]
    po[8:16, :] = own[:, RANK:2 * RANK]

    for cp in s3:
        cp.wait_recv()
    m0 = mall[:, :, 0:8, :].reshape(128, 128)
    m1 = mall[:, :, 8:16, :].reshape(128, 128)
    q = (jnp.dot(pt[:, 0:128], m0, precision=HIGHEST, preferred_element_type=jnp.float32)
         + jnp.dot(pt[:, 128:256], m1, precision=HIGHEST, preferred_element_type=jnp.float32)) * (1.0 / 32.0)

    def same(g, start, rows, device):
        part = qb.at[g, c, pl.ds(start, rows)]
        return go(part, part, device)

    qb[x, c, 0:RANK] = q
    qy = {}
    for d in (4, 1, 7, 2, 6, 3, 5):
        qy[d] = go(qb.at[x, c, pl.ds(0, RANK)], qb.at[x, c, pl.ds(ORDER.index(d) * RANK, RANK)], at_y(d))
    batches = ((0, 32, 16), (32, 64, 32), (96, 64, 32), (160, 96, 48))
    right, left, halves, qc = [], [], [], []

    def pass_on(k):
        start, rows, _ = batches[k]
        for d in ORDER[start // RANK:(start + rows) // RANK]:
            if d:
                qy[d].wait_recv()
        right.append(same(x, start, rows, at_x(1)))
        left.append(same(x, start, rows, at_x(3)))

    def relay_on(k):
        start, rows, first = batches[k]
        right[k].wait_recv()
        halves.append(same(ahead[3], start, first, at_x(1)))
        left[k].wait_recv()
        halves.append(same(ahead[1], start + first, rows - first, at_x(3)))

    for k in range(4):
        pass_on(k)
    for k in range(4):
        relay_on(k)
    qc.append(same(x, 0, 256, other))
    qc.append(same(ahead[3], 0, 256, other))
    qc.append(same(ahead[1], 0, 256, other))
    for cp in halves:
        cp.wait_recv()
    qc.append(same(ahead[2], 0, 256, other))
    for cp in qc:
        cp.wait_recv()
    for cp in started:
        cp.wait_send()


def apply(po, qb, grads, error, momentum, weight, new_error, new_momentum, new_weight, q_next, qt, ebuf, mbuf, wbuf, sem):
    y = lax.div(lax.axis_index("replica"), NX)
    copies = []
    width = 2048
    for g in range(D // width):
        for c in range(NC):
            for k, d in enumerate(ORDER):
                col = g * width + c * 1024 + lax.rem(y + (NY - d), NY) * 128
                qt[:, pl.ds(pl.multiple_of(col, 128), 128)] = qb[g, c, k * RANK:(k + 1) * RANK]
        cols = pl.ds(g * width, width)
        cp = pltpu.make_async_copy(qt.at[:, cols], q_next.at[:, cols], sem.at[12 + g])
        cp.start()
        copies.append(cp)
        approx = jnp.dot(po[...], qt[:, cols], precision=HIGHEST, preferred_element_type=jnp.float32)
        ebuf[:, cols] = (grads[:, cols].astype(jnp.float32) + error[:, cols]) - approx
        moved = 0.9 * momentum[:, cols] + approx
        mbuf[:, cols] = moved
        wbuf[:, cols] = (weight[:, cols].astype(jnp.float32) - 0.5 * moved).astype(jnp.bfloat16)
        for k, (src, dst) in enumerate(((ebuf, new_error), (mbuf, new_momentum), (wbuf, new_weight))):
            cp = pltpu.make_async_copy(src.at[:, cols], dst.at[:, cols], sem.at[g * 3 + k])
            cp.start()
            copies.append(cp)
    for cp in copies:
        cp.wait()


def on_device(grads, error, momentum, weight, q_start):
    f32 = jnp.float32
    rows = grads.shape[1]
    vmem = pltpu.VMEM
    blocks, p_ortho = pl.pallas_call(
        kernel,
        out_shape=(jax.ShapeDtypeStruct((NX, NC, NY * RANK, 128), f32), jax.ShapeDtypeStruct((rows, RANK), f32)),
        in_specs=[pl.BlockSpec(memory_space=pltpu.HBM)] * 3,
        out_specs=[pl.BlockSpec(memory_space=pltpu.VMEM)] * 2,
        scratch_shapes=[
            vmem((NX, rows, 2048), jnp.bfloat16),
            vmem((NX, rows, 2048), f32),
            vmem((NX, RANK, 2048), f32),
            vmem((NX, rows, 2048), f32),
            vmem((2, rows, 2048), f32),
            vmem((2, 8, 2048), f32),
            vmem((2, 8, 2048), f32),
            vmem((NY, NC, rows, 128), f32),
            vmem((NY - 1, NC, rows, 128), f32),
            vmem((NC, rows, 128), f32),
            vmem((NZ, NC, rows, 128), f32),
            vmem((8, 128), f32),
            vmem((8, 128), f32),
            vmem((NX, 8, 128), f32),
            vmem((NY, 8, 128), f32),
            vmem((NZ, NC, 8, 128), f32),
            vmem((128, 128), f32),
            pltpu.SemaphoreType.DMA((12,)),
            pltpu.SemaphoreType.DMA((96,)),
            pltpu.SemaphoreType.DMA((96,)),
        ],
        compiler_params=pltpu.CompilerParams(collective_id=0, has_side_effects=True, vmem_limit_bytes=24 * 2**20),
        name="reduce_factor_gather",
    )(*[pltpu.with_memory_space_constraint(a, pltpu.HBM) for a in (grads[0], error[0], q_start.T)])
    new_error, new_momentum, new_weight, q_next = pl.pallas_call(
        apply,
        out_shape=(
            jax.ShapeDtypeStruct((rows, D), f32),
            jax.ShapeDtypeStruct((rows, D), f32),
            jax.ShapeDtypeStruct((rows, D), jnp.bfloat16),
            jax.ShapeDtypeStruct((RANK, D), f32),
        ),
        in_specs=[pl.BlockSpec(memory_space=pltpu.VMEM)] * 6,
        out_specs=[pl.BlockSpec(memory_space=pl.ANY)] * 4,
        scratch_shapes=[
            vmem((RANK, D), f32),
            vmem((rows, D), f32),
            vmem((rows, D), f32),
            vmem((rows, D), jnp.bfloat16),
            pltpu.SemaphoreType.DMA((16,)),
        ],
        compiler_params=pltpu.CompilerParams(vmem_limit_bytes=24 * 2**20),
        name="apply",
    )(p_ortho, blocks, grads[0], error[0], momentum, weight)
    return (new_error[None], new_momentum, new_weight, q_next.T)


def solution(mesh):
    placed = (
        P("replica", "shard", None),
        P("replica", "shard", None),
        P("shard", None),
        P("shard", None),
        P(),
    )
    return jax.shard_map(
        on_device,
        mesh=mesh,
        in_specs=placed,
        out_specs=(P("replica", "shard", None), P("shard", None), P("shard", None), P()),
        check_vma=False,
    )
```

```python
import jax
import jax.numpy as jnp
from jax import lax
from jax.experimental import pallas as pl
from jax.experimental.pallas import tpu as pltpu
from jax.sharding import PartitionSpec as P

MESH = pl.DeviceIdType.MESH
HIGHEST = lax.Precision.HIGHEST
NX, NY, NZ, NC = 4, 8, 8, 2
RANK = 32
D = 8192
NT = (((1,), (1,)), ((), ()))
FAR8, FAR4 = (4, 3, 5, 2, 6, 1, 7), (2, 1, 3)
ORDER = (0, 1, 7, 2, 6, 3, 4, 5)


def send(src, dst, send_sem, recv_sem, device):
    copy = pltpu.make_async_remote_copy(
        src_ref=src, dst_ref=dst, send_sem=send_sem, recv_sem=recv_sem,
        device_id=device, device_id_type=MESH,
    )
    copy.start()
    return copy


def factor_rows(gram, pt, steps):
    sub = lax.broadcasted_iota(jnp.int32, (RANK, 1), 0)
    for j in steps:
        col = gram[:, j:j + 1]
        r = lax.rsqrt(gram[j:j + 1, j:j + 1])
        f = jnp.where(sub > j, col * r, 0.0)
        grow = gram[j:j + 1, :] * r
        prow = pt[j:j + 1, :] * r
        gram = gram - f * grow
        pt = jnp.where(sub == j, prow, pt - f * prow)
    return gram, pt


def kernel(grads, error, qs, qb, po, gbuf, ebuf, qsv, mbuf, s1buf, relay, passed, s1sum, s2buf, msum, mall,
           ploc, pysum, pxbuf, pybuf, pall, oscr, load_sem, ssem, rsem):
    rep, shard = lax.axis_index("replica"), lax.axis_index("shard")
    x, y = lax.rem(rep, NX), lax.div(rep, NX)
    c, z = lax.rem(shard, NC), lax.div(shard, NC)

    def at_x(d):
        return (y * NX + lax.rem(x + d, NX), shard)

    def at_y(d):
        return (lax.rem(y + d, NY) * NX + x, shard)

    def at_z(d):
        return (rep, lax.rem(z + d, NZ) * NC + c)

    def at_zc(d):
        return (rep, lax.rem(z + d, NZ) * NC + (1 - c))

    other = at_zc(0)

    slots = iter(range(128))
    started = []

    def go(src, dst, device):
        k = next(slots)
        copy = send(src, dst, ssem.at[k], rsem.at[k], device)
        started.append(copy)
        return copy

    ahead = [lax.rem(x + d, NX) for d in range(NX)]
    order = (2, 1, 3, 0)

    def load(src, dst, k, g):
        cp = pltpu.make_async_copy(src.at[:, pl.ds(pl.multiple_of(g * 2048, 2048), 2048)], dst.at[g], load_sem.at[k])
        cp.start()
        return cp

    barrier = pltpu.get_barrier_semaphore()
    partners = [at(d) for d in FAR8 for at in (at_y, at_z, at_zc)] + [other]
    partners = partners[:9] + [at_x(d) for d in FAR4] + partners[9:]

    def signal(some):
        for device in some:
            pl.semaphore_signal(barrier, inc=1, device_id=device, device_id_type=MESH)

    signal(partners[:10])
    mloads = [(load(grads, gbuf, i, ahead[d]), load(error, ebuf, 4 + i, ahead[d])) for i, d in enumerate(order)]
    signal(partners[10:])
    qloads = [load(qs, qsv, 8 + i, ahead[d]) for i, d in enumerate(order)]

    for i, d in enumerate(order):
        for cp in mloads[i]:
            cp.wait()
        mbuf[ahead[d]] = gbuf[ahead[d]].astype(jnp.float32) + ebuf[ahead[d]]

    lo, hi = pl.ds(0, 8), pl.ds(8, 8)
    pl.semaphore_wait(barrier, len(partners))
    parts = [pl.ds(k * 1024, 1024) for k in range(2)]
    relays = [(go(mbuf.at[ahead[2], lo, part], relay.at[0, :, part], at_x(1)),
               go(mbuf.at[ahead[2], hi, part], relay.at[1, :, part], at_x(3))) for part in parts]
    right_own = go(mbuf.at[ahead[1], hi], s1buf.at[0, hi], at_x(1))
    left_own = go(mbuf.at[ahead[3], lo], s1buf.at[1, lo], at_x(3))

    p = None
    for i, d in enumerate(order):
        qloads[i].wait()
        t = lax.dot_general(mbuf[ahead[d]], qsv[ahead[d]], NT, precision=HIGHEST, preferred_element_type=jnp.float32)
        p = t if p is None else p + t
    packed = jnp.concatenate([p[0:8], p[8:16], jnp.zeros((8, 64), jnp.float32)], axis=1)
    ploc[...] = packed
    py = [go(ploc, pybuf.at[y], at_y(d)) for d in FAR8]
    pybuf[y] = packed

    sums = []
    for k, part in enumerate(parts):
        for side, (g, rows, device) in enumerate(((ahead[1], lo, at_x(1)), (ahead[3], hi, at_x(3)))):
            relays[k][side].wait_recv()
            passed[side, :, part] = mbuf[g, rows, part] + relay[side, :, part]
            sums.append(go(passed.at[side, :, part], s1buf.at[side, rows, part], device))

    for cp in py:
        cp.wait_recv()
    packed = ((pybuf[0] + pybuf[1]) + (pybuf[2] + pybuf[3])) + ((pybuf[4] + pybuf[5]) + (pybuf[6] + pybuf[7]))
    pysum[...] = packed
    px = [go(pysum, pxbuf.at[x], at_x(d)) for d in FAR4]
    pxbuf[x] = packed

    for cp in [right_own, left_own] + sums:
        cp.wait_recv()
    for k in range(NY):
        for h in range(2):
            cols = pl.ds(h * 1024 + k * 128, 128)
            s1sum[k, h] = mbuf[x, :, cols] + (s1buf[0, :, cols] + s1buf[1, :, cols])
    s2 = [go(s1sum.at[lax.rem(y + d, NY)], s2buf.at[d - 1], at_y(d)) for d in FAR8]

    for cp in px:
        cp.wait_recv()
    pall[z, c] = (pxbuf[0] + pxbuf[1]) + (pxbuf[2] + pxbuf[3])
    pz = [go(pall.at[z, c], pall.at[z, c], at(d)) for d in FAR8 for at in (at_zc, at_z)] + [go(pall.at[z, c], pall.at[z, c], other)]

    for cp in s2:
        cp.wait_recv()
    total = s1sum[y]
    for k in range(NY - 1):
        total = total + s2buf[k]
    msum[...] = total
    mall[z, c] = msum[c]
    s3 = [go(msum.at[h], mall.at[z, c], at(d)) for d in FAR8 for h, at in ((1 - c, at_zc), (c, at_z))]
    s3.append(go(msum.at[1 - c], mall.at[z, c], other))

    for cp in pz:
        cp.wait_recv()
    pt = pall[...].reshape(128, 128).T
    p0, p1 = pt[0:RANK], pt[RANK:2 * RANK]
    gram = (lax.dot_general(p0, p0, NT, precision=HIGHEST, preferred_element_type=jnp.float32)
            + lax.dot_general(p1, p1, NT, precision=HIGHEST, preferred_element_type=jnp.float32))
    pt = jnp.concatenate([p0, p1], axis=1)
    gram, pt = factor_rows(gram, pt, range(RANK))
    ot = jnp.concatenate([pt[:, 0:128], pt[:, 128:256], jnp.zeros((64, 128), jnp.float32)], axis=0)
    oscr[...] = ot.T
    own = oscr[pl.ds(pl.multiple_of(shard * 8, 8), 8), :]
    po[0:8, :] = own[:, 0:RANK]
    po[8:16, :] = own[:, RANK:2 * RANK]

    for cp in s3:
        cp.wait_recv()
    m0 = mall[:, :, 0:8, :].reshape(128, 128)
    m1 = mall[:, :, 8:16, :].reshape(128, 128)
    q = (jnp.dot(pt[:, 0:128], m0, precision=HIGHEST, preferred_element_type=jnp.float32)
         + jnp.dot(pt[:, 128:256], m1, precision=HIGHEST, preferred_element_type=jnp.float32)) * (1.0 / 32.0)

    def same(g, start, rows, device):
        part = qb.at[g, c, pl.ds(start, rows)]
        return go(part, part, device)

    qb[x, c, 0:RANK] = q
    qy = {}
    for d in (1, 7, 2, 6, 4, 3, 5):
        qy[d] = go(qb.at[x, c, pl.ds(0, RANK)], qb.at[x, c, pl.ds(ORDER.index(d) * RANK, RANK)], at_y(d))
    batches = ((0, 32), (32, 64), (96, 64), (160, 96))
    qx = []
    for start, rows in batches:
        for d in ORDER[start // RANK:(start + rows) // RANK]:
            if d:
                qy[d].wait_recv()
        qx.append([same(x, start, rows, at_x(d)) for d in FAR4])
    qc = [same(x, 0, 256, other)]
    for some, start, rows in ((qx[:3], 0, 160), (qx[3:], 160, 96)):
        for k, d in enumerate(FAR4):
            for sent in some:
                sent[k].wait_recv()
            qc.append(same(ahead[NX - d], start, rows, other))
    for cp in qc:
        cp.wait_recv()
    for cp in started:
        cp.wait_send()


def apply(po, qb, grads, error, momentum, weight, new_error, new_momentum, new_weight, q_next, qt, ebuf, mbuf, wbuf, sem):
    y = lax.div(lax.axis_index("replica"), NX)
    copies = []
    width = 2048
    for g in range(D // width):
        for c in range(NC):
            for k, d in enumerate(ORDER):
                col = g * width + c * 1024 + lax.rem(y + (NY - d), NY) * 128
                qt[:, pl.ds(pl.multiple_of(col, 128), 128)] = qb[g, c, k * RANK:(k + 1) * RANK]
        cols = pl.ds(g * width, width)
        cp = pltpu.make_async_copy(qt.at[:, cols], q_next.at[:, cols], sem.at[12 + g])
        cp.start()
        copies.append(cp)
        approx = jnp.dot(po[...], qt[:, cols], precision=HIGHEST, preferred_element_type=jnp.float32)
        ebuf[:, cols] = (grads[:, cols].astype(jnp.float32) + error[:, cols]) - approx
        moved = 0.9 * momentum[:, cols] + approx
        mbuf[:, cols] = moved
        wbuf[:, cols] = (weight[:, cols].astype(jnp.float32) - 0.5 * moved).astype(jnp.bfloat16)
        for k, (src, dst) in enumerate(((ebuf, new_error), (mbuf, new_momentum), (wbuf, new_weight))):
            cp = pltpu.make_async_copy(src.at[:, cols], dst.at[:, cols], sem.at[g * 3 + k])
            cp.start()
            copies.append(cp)
    for cp in copies:
        cp.wait()


def on_device(grads, error, momentum, weight, q_start):
    f32 = jnp.float32
    rows = grads.shape[1]
    vmem = pltpu.VMEM
    blocks, p_ortho = pl.pallas_call(
        kernel,
        out_shape=(jax.ShapeDtypeStruct((NX, NC, NY * RANK, 128), f32), jax.ShapeDtypeStruct((rows, RANK), f32)),
        in_specs=[pl.BlockSpec(memory_space=pltpu.HBM)] * 3,
        out_specs=[pl.BlockSpec(memory_space=pltpu.VMEM)] * 2,
        scratch_shapes=[
            vmem((NX, rows, 2048), jnp.bfloat16),
            vmem((NX, rows, 2048), f32),
            vmem((NX, RANK, 2048), f32),
            vmem((NX, rows, 2048), f32),
            vmem((2, rows, 2048), f32),
            vmem((2, 8, 2048), f32),
            vmem((2, 8, 2048), f32),
            vmem((NY, NC, rows, 128), f32),
            vmem((NY - 1, NC, rows, 128), f32),
            vmem((NC, rows, 128), f32),
            vmem((NZ, NC, rows, 128), f32),
            vmem((8, 128), f32),
            vmem((8, 128), f32),
            vmem((NX, 8, 128), f32),
            vmem((NY, 8, 128), f32),
            vmem((NZ, NC, 8, 128), f32),
            vmem((128, 128), f32),
            pltpu.SemaphoreType.DMA((12,)),
            pltpu.SemaphoreType.DMA((96,)),
            pltpu.SemaphoreType.DMA((96,)),
        ],
        compiler_params=pltpu.CompilerParams(collective_id=0, has_side_effects=True, vmem_limit_bytes=24 * 2**20),
        name="reduce_factor_gather",
    )(*[pltpu.with_memory_space_constraint(a, pltpu.HBM) for a in (grads[0], error[0], q_start.T)])
    new_error, new_momentum, new_weight, q_next = pl.pallas_call(
        apply,
        out_shape=(
            jax.ShapeDtypeStruct((rows, D), f32),
            jax.ShapeDtypeStruct((rows, D), f32),
            jax.ShapeDtypeStruct((rows, D), jnp.bfloat16),
            jax.ShapeDtypeStruct((RANK, D), f32),
        ),
        in_specs=[pl.BlockSpec(memory_space=pltpu.VMEM)] * 6,
        out_specs=[pl.BlockSpec(memory_space=pl.ANY)] * 4,
        scratch_shapes=[
            vmem((RANK, D), f32),
            vmem((rows, D), f32),
            vmem((rows, D), f32),
            vmem((rows, D), jnp.bfloat16),
            pltpu.SemaphoreType.DMA((16,)),
        ],
        compiler_params=pltpu.CompilerParams(vmem_limit_bytes=24 * 2**20),
        name="apply",
    )(p_ortho, blocks, grads[0], error[0], momentum, weight)
    return (new_error[None], new_momentum, new_weight, q_next.T)


def solution(mesh):
    placed = (
        P("replica", "shard", None),
        P("replica", "shard", None),
        P("shard", None),
        P("shard", None),
        P(),
    )
    return jax.shard_map(
        on_device,
        mesh=mesh,
        in_specs=placed,
        out_specs=(P("replica", "shard", None), P("shard", None), P("shard", None), P()),
        check_vma=False,
    )
```

```python
import jax
import jax.numpy as jnp
from jax import lax
from jax.experimental import pallas as pl
from jax.experimental.pallas import tpu as pltpu
from jax.sharding import PartitionSpec as P

MESH = pl.DeviceIdType.MESH
HIGHEST = lax.Precision.HIGHEST
NX, NY, NZ, NC = 4, 8, 8, 2
RANK = 32
D = 8192
NT = (((1,), (1,)), ((), ()))
FAR8, FAR4 = (4, 3, 5, 2, 6, 1, 7), (2, 1, 3)
ORDER = (0, 1, 7, 2, 6, 3, 4, 5)


def send(src, dst, send_sem, recv_sem, device):
    copy = pltpu.make_async_remote_copy(
        src_ref=src, dst_ref=dst, send_sem=send_sem, recv_sem=recv_sem,
        device_id=device, device_id_type=MESH,
    )
    copy.start()
    return copy


def factor_rows(gram, pt, steps):
    sub = lax.broadcasted_iota(jnp.int32, (RANK, 1), 0)
    for j in steps:
        col = gram[:, j:j + 1]
        r = lax.rsqrt(gram[j:j + 1, j:j + 1])
        f = jnp.where(sub > j, col * r, 0.0)
        grow = gram[j:j + 1, :] * r
        prow = pt[j:j + 1, :] * r
        gram = gram - f * grow
        pt = jnp.where(sub == j, prow, pt - f * prow)
    return gram, pt


def kernel(grads, error, qs, qb, po, mbuf, gbuf, ebuf, qsv, s1buf, relay, passed, s1sum, s2buf, msum, mall,
           ploc, pysum, pxbuf, pybuf, pall, oscr, load_sem, ssem, rsem):
    rep, shard = lax.axis_index("replica"), lax.axis_index("shard")
    x, y = lax.rem(rep, NX), lax.div(rep, NX)
    c, z = lax.rem(shard, NC), lax.div(shard, NC)

    def at_x(d):
        return (y * NX + lax.rem(x + d, NX), shard)

    def at_y(d):
        return (lax.rem(y + d, NY) * NX + x, shard)

    def at_z(d):
        return (rep, lax.rem(z + d, NZ) * NC + c)

    def at_zc(d):
        return (rep, lax.rem(z + d, NZ) * NC + (1 - c))

    other = at_zc(0)

    slots = iter(range(128))
    started = []

    def go(src, dst, device):
        k = next(slots)
        copy = send(src, dst, ssem.at[k], rsem.at[k], device)
        started.append(copy)
        return copy

    ahead = [lax.rem(x + d, NX) for d in range(NX)]
    order = (2, 1, 3, 0)

    def load(src, dst, k, g):
        cp = pltpu.make_async_copy(src.at[:, pl.ds(pl.multiple_of(g * 2048, 2048), 2048)], dst.at[g], load_sem.at[k])
        cp.start()
        return cp

    barrier = pltpu.get_barrier_semaphore()
    partners = [at(d) for d in FAR8 for at in (at_y, at_z, at_zc)] + [other]
    partners = partners[:9] + [at_x(d) for d in FAR4] + partners[9:]

    def signal(some):
        for device in some:
            pl.semaphore_signal(barrier, inc=1, device_id=device, device_id_type=MESH)

    signal(partners[:10])
    mloads = [(load(grads, gbuf, i, ahead[d]), load(error, ebuf, 4 + i, ahead[d])) for i, d in enumerate(order)]
    signal(partners[10:])
    qloads = [load(qs, qsv, 8 + i, ahead[d]) for i, d in enumerate(order)]

    for i, d in enumerate(order):
        for cp in mloads[i]:
            cp.wait()
        mbuf[ahead[d]] = gbuf[ahead[d]].astype(jnp.float32) + ebuf[ahead[d]]

    lo, hi = pl.ds(0, 8), pl.ds(8, 8)
    pl.semaphore_wait(barrier, len(partners))
    parts = [pl.ds(k * 1024, 1024) for k in range(2)]
    relays = [(go(mbuf.at[ahead[2], lo, part], relay.at[0, :, part], at_x(1)),
               go(mbuf.at[ahead[2], hi, part], relay.at[1, :, part], at_x(3))) for part in parts]
    right_own = go(mbuf.at[ahead[1], hi], s1buf.at[0, hi], at_x(1))
    left_own = go(mbuf.at[ahead[3], lo], s1buf.at[1, lo], at_x(3))

    p = None
    for i, d in enumerate(order):
        qloads[i].wait()
        t = lax.dot_general(mbuf[ahead[d]], qsv[ahead[d]], NT, precision=HIGHEST, preferred_element_type=jnp.float32)
        p = t if p is None else p + t
    packed = jnp.concatenate([p[0:8], p[8:16], jnp.zeros((8, 64), jnp.float32)], axis=1)
    ploc[...] = packed
    py = [go(ploc, pybuf.at[y], at_y(d)) for d in FAR8]
    pybuf[y] = packed

    sums = []
    for k, part in enumerate(parts):
        for side, (g, rows, device) in enumerate(((ahead[1], lo, at_x(1)), (ahead[3], hi, at_x(3)))):
            relays[k][side].wait_recv()
            passed[side, :, part] = mbuf[g, rows, part] + relay[side, :, part]
            sums.append(go(passed.at[side, :, part], s1buf.at[side, rows, part], device))

    for cp in py:
        cp.wait_recv()
    packed = ((pybuf[0] + pybuf[1]) + (pybuf[2] + pybuf[3])) + ((pybuf[4] + pybuf[5]) + (pybuf[6] + pybuf[7]))
    pysum[...] = packed
    px = [go(pysum, pxbuf.at[x], at_x(d)) for d in FAR4]
    pxbuf[x] = packed

    for cp in [right_own, left_own] + sums:
        cp.wait_recv()
    for k in range(NY):
        for h in range(2):
            cols = pl.ds(h * 1024 + k * 128, 128)
            s1sum[k, h] = mbuf[x, :, cols] + (s1buf[0, :, cols] + s1buf[1, :, cols])
    s2 = [go(s1sum.at[lax.rem(y + d, NY)], s2buf.at[d - 1], at_y(d)) for d in FAR8]

    for cp in px:
        cp.wait_recv()
    pall[z, c] = (pxbuf[0] + pxbuf[1]) + (pxbuf[2] + pxbuf[3])
    pz = [go(pall.at[z, c], pall.at[z, c], at(d)) for d in FAR8 for at in (at_zc, at_z)] + [go(pall.at[z, c], pall.at[z, c], other)]

    for cp in s2:
        cp.wait_recv()
    total = s1sum[y]
    for k in range(NY - 1):
        total = total + s2buf[k]
    msum[...] = total
    mall[z, c] = msum[c]
    s3 = [go(msum.at[h], mall.at[z, c], at(d)) for d in FAR8 for h, at in ((1 - c, at_zc), (c, at_z))]
    s3.append(go(msum.at[1 - c], mall.at[z, c], other))

    for cp in pz:
        cp.wait_recv()
    pt = pall[...].reshape(128, 128).T
    p0, p1 = pt[0:RANK], pt[RANK:2 * RANK]
    gram = (lax.dot_general(p0, p0, NT, precision=HIGHEST, preferred_element_type=jnp.float32)
            + lax.dot_general(p1, p1, NT, precision=HIGHEST, preferred_element_type=jnp.float32))
    pt = jnp.concatenate([p0, p1], axis=1)
    gram, pt = factor_rows(gram, pt, range(RANK))
    for cp in s3:
        cp.wait_recv()
    m = jnp.concatenate([mall[:, :, 0:8, :].reshape(128, 128), mall[:, :, 8:16, :].reshape(128, 128)], axis=0)
    q = jnp.dot(pt, m, precision=HIGHEST, preferred_element_type=jnp.float32) * (1.0 / 32.0)

    def same(g, start, rows, device):
        part = qb.at[g, c, pl.ds(start, rows)]
        return go(part, part, device)

    qb[x, c, 0:RANK] = q
    before = len(started)
    qy = {}
    for d in (1, 7, 2, 6, 4, 3, 5):
        qy[d] = go(qb.at[x, c, pl.ds(0, RANK)], qb.at[x, c, pl.ds(ORDER.index(d) * RANK, RANK)], at_y(d))
    batches = ((0, 32), (32, 64), (96, 64), (160, 96))
    qx = [[same(x, 0, RANK, at_x(d)) for d in FAR4]]
    ot = jnp.concatenate([pt[:, 0:128], pt[:, 128:256], jnp.zeros((64, 128), jnp.float32)], axis=0)
    oscr[...] = ot.T
    own = oscr[pl.ds(pl.multiple_of(shard * 8, 8), 8), :]
    po[0:8, :] = own[:, 0:RANK]
    po[8:16, :] = own[:, RANK:2 * RANK]
    for cp in started[:before]:
        cp.wait_send()
    for start, rows in batches[1:]:
        for d in ORDER[start // RANK:(start + rows) // RANK]:
            qy[d].wait_recv()
        qx.append([same(x, start, rows, at_x(d)) for d in FAR4])
    qc = [same(x, 0, 256, other)]
    for some, start, rows in ((qx[:3], 0, 160), (qx[3:], 160, 96)):
        for k, d in enumerate(FAR4):
            for sent in some:
                sent[k].wait_recv()
            qc.append(same(ahead[NX - d], start, rows, other))
    for cp in started[before:-1]:
        cp.wait_send()
    for cp in qc:
        cp.wait_recv()
    started[-1].wait_send()


def apply(po, qb, merged, momentum, weight, new_error, new_momentum, new_weight, q_next, qt, ebuf, mbuf, wbuf, sem):
    y = lax.div(lax.axis_index("replica"), NX)
    copies = []
    width = 2048
    for g in range(D // width):
        for c in range(NC):
            for k, d in enumerate(ORDER):
                col = g * width + c * 1024 + lax.rem(y + (NY - d), NY) * 128
                qt[:, pl.ds(pl.multiple_of(col, 128), 128)] = qb[g, c, k * RANK:(k + 1) * RANK]
        cols = pl.ds(g * width, width)
        cp = pltpu.make_async_copy(qt.at[:, cols], q_next.at[:, cols], sem.at[12 + g])
        cp.start()
        copies.append(cp)
        approx = jnp.dot(po[...], qt[:, cols], precision=HIGHEST, preferred_element_type=jnp.float32)
        ebuf[:, cols] = merged[g] - approx
        moved = 0.9 * momentum[:, cols] + approx
        mbuf[:, cols] = moved
        wbuf[:, cols] = (weight[:, cols].astype(jnp.float32) - 0.5 * moved).astype(jnp.bfloat16)
        for k, (src, dst) in enumerate(((ebuf, new_error), (mbuf, new_momentum), (wbuf, new_weight))):
            cp = pltpu.make_async_copy(src.at[:, cols], dst.at[:, cols], sem.at[g * 3 + k])
            cp.start()
            copies.append(cp)
    for cp in copies:
        cp.wait()


def on_device(grads, error, momentum, weight, q_start):
    f32 = jnp.float32
    rows = grads.shape[1]
    vmem = pltpu.VMEM
    blocks, p_ortho, merged = pl.pallas_call(
        kernel,
        out_shape=(jax.ShapeDtypeStruct((NX, NC, NY * RANK, 128), f32), jax.ShapeDtypeStruct((rows, RANK), f32),
                   jax.ShapeDtypeStruct((NX, rows, 2048), f32)),
        in_specs=[pl.BlockSpec(memory_space=pltpu.HBM)] * 3,
        out_specs=[pl.BlockSpec(memory_space=pltpu.VMEM)] * 3,
        scratch_shapes=[
            vmem((NX, rows, 2048), jnp.bfloat16),
            vmem((NX, rows, 2048), f32),
            vmem((NX, RANK, 2048), f32),
            vmem((2, rows, 2048), f32),
            vmem((2, 8, 2048), f32),
            vmem((2, 8, 2048), f32),
            vmem((NY, NC, rows, 128), f32),
            vmem((NY - 1, NC, rows, 128), f32),
            vmem((NC, rows, 128), f32),
            vmem((NZ, NC, rows, 128), f32),
            vmem((8, 128), f32),
            vmem((8, 128), f32),
            vmem((NX, 8, 128), f32),
            vmem((NY, 8, 128), f32),
            vmem((NZ, NC, 8, 128), f32),
            vmem((128, 128), f32),
            pltpu.SemaphoreType.DMA((12,)),
            pltpu.SemaphoreType.DMA((96,)),
            pltpu.SemaphoreType.DMA((96,)),
        ],
        compiler_params=pltpu.CompilerParams(collective_id=0, has_side_effects=True, vmem_limit_bytes=24 * 2**20),
        name="reduce_factor_gather",
    )(*[pltpu.with_memory_space_constraint(a, pltpu.HBM) for a in (grads[0], error[0], q_start.T)])
    new_error, new_momentum, new_weight, q_next = pl.pallas_call(
        apply,
        out_shape=(
            jax.ShapeDtypeStruct((rows, D), f32),
            jax.ShapeDtypeStruct((rows, D), f32),
            jax.ShapeDtypeStruct((rows, D), jnp.bfloat16),
            jax.ShapeDtypeStruct((RANK, D), f32),
        ),
        in_specs=[pl.BlockSpec(memory_space=pltpu.VMEM)] * 5,
        out_specs=[pl.BlockSpec(memory_space=pl.ANY)] * 4,
        scratch_shapes=[
            vmem((RANK, D), f32),
            vmem((rows, D), f32),
            vmem((rows, D), f32),
            vmem((rows, D), jnp.bfloat16),
            pltpu.SemaphoreType.DMA((16,)),
        ],
        compiler_params=pltpu.CompilerParams(vmem_limit_bytes=24 * 2**20),
        name="apply",
    )(p_ortho, blocks, merged, momentum, weight)
    return (new_error[None], new_momentum, new_weight, q_next.T)


def solution(mesh):
    placed = (
        P("replica", "shard", None),
        P("replica", "shard", None),
        P("shard", None),
        P("shard", None),
        P(),
    )
    return jax.shard_map(
        on_device,
        mesh=mesh,
        in_specs=placed,
        out_specs=(P("replica", "shard", None), P("shard", None), P("shard", None), P()),
        check_vma=False,
    )
```

```python
import jax
import jax.numpy as jnp
from jax import lax
from jax.experimental import pallas as pl
from jax.experimental.pallas import tpu as pltpu
from jax.sharding import PartitionSpec as P

MESH = pl.DeviceIdType.MESH
HIGHEST = lax.Precision.HIGHEST
NX, NY, NZ, NC = 4, 8, 8, 2
RANK = 32
D = 8192
NT = (((1,), (1,)), ((), ()))
FAR8, FAR4 = (4, 3, 5, 2, 6, 1, 7), (2, 1, 3)
ORDER = (0, 1, 7, 2, 6, 3, 4, 5)


def send(src, dst, send_sem, recv_sem, device):
    copy = pltpu.make_async_remote_copy(
        src_ref=src, dst_ref=dst, send_sem=send_sem, recv_sem=recv_sem,
        device_id=device, device_id_type=MESH,
    )
    copy.start()
    return copy


def factor_rows(gram, pt, steps):
    sub = lax.broadcasted_iota(jnp.int32, (RANK, 1), 0)
    for j in steps:
        col = gram[:, j:j + 1]
        r = lax.rsqrt(gram[j:j + 1, j:j + 1])
        f = jnp.where(sub > j, col * r, 0.0)
        grow = gram[j:j + 1, :] * r
        prow = pt[j:j + 1, :] * r
        gram = gram - f * grow
        pt = jnp.where(sub == j, prow, pt - f * prow)
    return gram, pt


def kernel(grads, error, qs, qb, po, mbuf, gbuf, ebuf, qsv, s1buf, relay, passed, s1sum, s2buf, msum, mall,
           ploc, pysum, pxbuf, pybuf, pall, oscr, load_sem, ssem, rsem):
    rep, shard = lax.axis_index("replica"), lax.axis_index("shard")
    x, y = lax.rem(rep, NX), lax.div(rep, NX)
    c, z = lax.rem(shard, NC), lax.div(shard, NC)

    def at_x(d):
        return (y * NX + lax.rem(x + d, NX), shard)

    def at_y(d):
        return (lax.rem(y + d, NY) * NX + x, shard)

    def at_z(d):
        return (rep, lax.rem(z + d, NZ) * NC + c)

    def at_zc(d):
        return (rep, lax.rem(z + d, NZ) * NC + (1 - c))

    other = at_zc(0)

    slots = iter(range(128))
    started = []

    def go(src, dst, device):
        k = next(slots)
        copy = send(src, dst, ssem.at[k], rsem.at[k], device)
        started.append(copy)
        return copy

    ahead = [lax.rem(x + d, NX) for d in range(NX)]
    order = (2, 1, 3, 0)

    def load(src, dst, k, g):
        cp = pltpu.make_async_copy(src.at[:, pl.ds(pl.multiple_of(g * 2048, 2048), 2048)], dst.at[g], load_sem.at[k])
        cp.start()
        return cp

    barrier = pltpu.get_barrier_semaphore()
    partners = [at(d) for d in FAR8 for at in (at_y, at_z, at_zc)] + [other]
    partners = partners[:9] + [at_x(d) for d in FAR4] + partners[9:]

    def signal(some):
        for device in some:
            pl.semaphore_signal(barrier, inc=1, device_id=device, device_id_type=MESH)

    signal(partners[:10])
    mloads = [(load(grads, gbuf, i, ahead[d]), load(error, ebuf, 4 + i, ahead[d])) for i, d in enumerate(order)]
    signal(partners[10:])
    qloads = [load(qs, qsv, 8 + i, ahead[d]) for i, d in enumerate(order)]

    for i, d in enumerate(order):
        for cp in mloads[i]:
            cp.wait()
        mbuf[ahead[d]] = gbuf[ahead[d]].astype(jnp.float32) + ebuf[ahead[d]]

    lo, hi = pl.ds(0, 8), pl.ds(8, 8)
    pl.semaphore_wait(barrier, len(partners))
    parts = [pl.ds(k * 1024, 1024) for k in range(2)]
    relays = [(go(mbuf.at[ahead[2], lo, part], relay.at[0, :, part], at_x(1)),
               go(mbuf.at[ahead[2], hi, part], relay.at[1, :, part], at_x(3))) for part in parts]
    right_own = go(mbuf.at[ahead[1], hi], s1buf.at[0, hi], at_x(1))
    left_own = go(mbuf.at[ahead[3], lo], s1buf.at[1, lo], at_x(3))

    p = None
    for i, d in enumerate(order):
        qloads[i].wait()
        t = lax.dot_general(mbuf[ahead[d]], qsv[ahead[d]], NT, precision=HIGHEST, preferred_element_type=jnp.float32)
        p = t if p is None else p + t
    packed = jnp.concatenate([p[0:8], p[8:16], jnp.zeros((8, 64), jnp.float32)], axis=1)
    ploc[...] = packed
    py = [go(ploc, pybuf.at[y], at_y(d)) for d in FAR8]
    pybuf[y] = packed

    sums = []
    for k, part in enumerate(parts):
        for side, (g, rows, device) in enumerate(((ahead[1], lo, at_x(1)), (ahead[3], hi, at_x(3)))):
            relays[k][side].wait_recv()
            passed[side, :, part] = mbuf[g, rows, part] + relay[side, :, part]
            sums.append(go(passed.at[side, :, part], s1buf.at[side, rows, part], device))

    for cp in py:
        cp.wait_recv()
    packed = ((pybuf[0] + pybuf[1]) + (pybuf[2] + pybuf[3])) + ((pybuf[4] + pybuf[5]) + (pybuf[6] + pybuf[7]))
    pysum[...] = packed
    px = [go(pysum, pxbuf.at[x], at_x(d)) for d in FAR4]
    pxbuf[x] = packed

    for cp in [right_own, left_own] + sums:
        cp.wait_recv()
    for k in range(NY):
        for h in range(2):
            cols = pl.ds(h * 1024 + k * 128, 128)
            s1sum[k, h] = mbuf[x, :, cols] + (s1buf[0, :, cols] + s1buf[1, :, cols])
    s2 = [go(s1sum.at[lax.rem(y + d, NY)], s2buf.at[d - 1], at_y(d)) for d in FAR8]

    for cp in px:
        cp.wait_recv()
    pall[z, c] = (pxbuf[0] + pxbuf[1]) + (pxbuf[2] + pxbuf[3])
    pz = [go(pall.at[z, c], pall.at[z, c], at(d)) for d in FAR8 for at in (at_zc, at_z)] + [go(pall.at[z, c], pall.at[z, c], other)]

    for cp in s2:
        cp.wait_recv()
    total = s1sum[y]
    for k in range(NY - 1):
        total = total + s2buf[k]
    msum[...] = total
    mall[z, c] = msum[c]
    s3 = [go(msum.at[h], mall.at[z, c], at(d)) for d in FAR8 for h, at in ((1 - c, at_zc), (c, at_z))]
    s3.append(go(msum.at[1 - c], mall.at[z, c], other))

    for cp in pz:
        cp.wait_recv()
    pt = pall[...].reshape(128, 128).T
    p0, p1 = pt[0:RANK], pt[RANK:2 * RANK]
    gram = (lax.dot_general(p0, p0, NT, precision=HIGHEST, preferred_element_type=jnp.float32)
            + lax.dot_general(p1, p1, NT, precision=HIGHEST, preferred_element_type=jnp.float32))
    pt = jnp.concatenate([p0, p1], axis=1)
    gram, pt = factor_rows(gram, pt, range(RANK))
    for cp in s3:
        cp.wait_recv()
    m = jnp.concatenate([mall[:, :, 0:8, :].reshape(128, 128), mall[:, :, 8:16, :].reshape(128, 128)], axis=0)
    q = jnp.dot(pt, m, precision=HIGHEST, preferred_element_type=jnp.float32) * (1.0 / 32.0)

    def same(g, start, rows, device):
        part = qb.at[g, c, pl.ds(start, rows)]
        return go(part, part, device)

    qb[x, c, 0:RANK] = q
    before = len(started)
    qy = {}
    for d in (1, 7, 2, 6, 4, 3, 5):
        qy[d] = go(qb.at[x, c, pl.ds(0, RANK)], qb.at[x, c, pl.ds(ORDER.index(d) * RANK, RANK)], at_y(d))
    batches = ((0, 32), (32, 64), (96, 64), (160, 96))
    qx = [[same(x, 0, RANK, at_x(d)) for d in FAR4]]
    ot = jnp.concatenate([pt[:, 0:128], pt[:, 128:256], jnp.zeros((64, 128), jnp.float32)], axis=0)
    oscr[...] = ot.T
    own = oscr[pl.ds(pl.multiple_of(shard * 8, 8), 8), :]
    po[0:8, :] = own[:, 0:RANK]
    po[8:16, :] = own[:, RANK:2 * RANK]
    for cp in started[:before]:
        cp.wait_send()
    for start, rows in batches[1:]:
        for d in ORDER[start // RANK:(start + rows) // RANK]:
            qy[d].wait_recv()
        qx.append([same(x, start, rows, at_x(d)) for d in FAR4])
    qc = [same(x, 0, 256, other)]
    for some, start, rows in ((qx[:3], 0, 160), (qx[3:], 160, 96)):
        for k, d in enumerate(FAR4):
            for sent in some:
                sent[k].wait_recv()
            qc.append(same(ahead[NX - d], start, rows, other))
    for cp in started[before:-1]:
        cp.wait_send()
    for cp in qc:
        cp.wait_recv()
    started[-1].wait_send()


def thirds(a):
    high = a.astype(jnp.bfloat16)
    rest = a - high.astype(jnp.float32)
    middle = rest.astype(jnp.bfloat16)
    return high, middle, (rest - middle.astype(jnp.float32)).astype(jnp.bfloat16)


def apply(po, qb, merged, momentum, weight, new_error, new_momentum, new_weight, q_next, qt, ebuf, mbuf, wbuf, sem):
    y = lax.div(lax.axis_index("replica"), NX)
    high, middle, low = thirds(po[...])
    left = jnp.concatenate([high, high, high, middle, middle, low], axis=1)
    copies = []
    width = 2048
    for g in range(D // width):
        for c in range(NC):
            for k, d in enumerate(ORDER):
                col = g * width + c * 1024 + lax.rem(y + (NY - d), NY) * 128
                qt[:, pl.ds(pl.multiple_of(col, 128), 128)] = qb[g, c, k * RANK:(k + 1) * RANK]
        cols = pl.ds(g * width, width)
        cp = pltpu.make_async_copy(qt.at[:, cols], q_next.at[:, cols], sem.at[12 + g])
        cp.start()
        copies.append(cp)
        high, middle, low = thirds(qt[:, cols])
        right = jnp.concatenate([high, middle, low, high, middle, high], axis=0)
        approx = jnp.dot(left, right, preferred_element_type=jnp.float32)
        ebuf[:, cols] = merged[g] - approx
        moved = 0.9 * momentum[:, cols] + approx
        mbuf[:, cols] = moved
        wbuf[:, cols] = (weight[:, cols].astype(jnp.float32) - 0.5 * moved).astype(jnp.bfloat16)
        for k, (src, dst) in enumerate(((ebuf, new_error), (mbuf, new_momentum), (wbuf, new_weight))):
            cp = pltpu.make_async_copy(src.at[:, cols], dst.at[:, cols], sem.at[g * 3 + k])
            cp.start()
            copies.append(cp)
    for cp in copies:
        cp.wait()


def on_device(grads, error, momentum, weight, q_start):
    f32 = jnp.float32
    rows = grads.shape[1]
    vmem = pltpu.VMEM
    blocks, p_ortho, merged = pl.pallas_call(
        kernel,
        out_shape=(jax.ShapeDtypeStruct((NX, NC, NY * RANK, 128), f32), jax.ShapeDtypeStruct((rows, RANK), f32),
                   jax.ShapeDtypeStruct((NX, rows, 2048), f32)),
        in_specs=[pl.BlockSpec(memory_space=pltpu.HBM)] * 3,
        out_specs=[pl.BlockSpec(memory_space=pltpu.VMEM)] * 3,
        scratch_shapes=[
            vmem((NX, rows, 2048), jnp.bfloat16),
            vmem((NX, rows, 2048), f32),
            vmem((NX, RANK, 2048), f32),
            vmem((2, rows, 2048), f32),
            vmem((2, 8, 2048), f32),
            vmem((2, 8, 2048), f32),
            vmem((NY, NC, rows, 128), f32),
            vmem((NY - 1, NC, rows, 128), f32),
            vmem((NC, rows, 128), f32),
            vmem((NZ, NC, rows, 128), f32),
            vmem((8, 128), f32),
            vmem((8, 128), f32),
            vmem((NX, 8, 128), f32),
            vmem((NY, 8, 128), f32),
            vmem((NZ, NC, 8, 128), f32),
            vmem((128, 128), f32),
            pltpu.SemaphoreType.DMA((12,)),
            pltpu.SemaphoreType.DMA((96,)),
            pltpu.SemaphoreType.DMA((96,)),
        ],
        compiler_params=pltpu.CompilerParams(collective_id=0, has_side_effects=True, vmem_limit_bytes=24 * 2**20),
        name="reduce_factor_gather",
    )(*[pltpu.with_memory_space_constraint(a, pltpu.HBM) for a in (grads[0], error[0], q_start.T)])
    new_error, new_momentum, new_weight, q_next = pl.pallas_call(
        apply,
        out_shape=(
            jax.ShapeDtypeStruct((rows, D), f32),
            jax.ShapeDtypeStruct((rows, D), f32),
            jax.ShapeDtypeStruct((rows, D), jnp.bfloat16),
            jax.ShapeDtypeStruct((RANK, D), f32),
        ),
        in_specs=[pl.BlockSpec(memory_space=pltpu.VMEM)] * 5,
        out_specs=[pl.BlockSpec(memory_space=pl.ANY)] * 4,
        scratch_shapes=[
            vmem((RANK, D), f32),
            vmem((rows, D), f32),
            vmem((rows, D), f32),
            vmem((rows, D), jnp.bfloat16),
            pltpu.SemaphoreType.DMA((16,)),
        ],
        compiler_params=pltpu.CompilerParams(vmem_limit_bytes=24 * 2**20),
        name="apply",
    )(p_ortho, blocks, merged, momentum, weight)
    return (new_error[None], new_momentum, new_weight, q_next.T)


def solution(mesh):
    placed = (
        P("replica", "shard", None),
        P("replica", "shard", None),
        P("shard", None),
        P("shard", None),
        P(),
    )
    return jax.shard_map(
        on_device,
        mesh=mesh,
        in_specs=placed,
        out_specs=(P("replica", "shard", None), P("shard", None), P("shard", None), P()),
        check_vma=False,
    )
```
